32 devices in a mesh: cols: 8 (over z, x), mem: 4 (over y, core).
Axes of the slice: x: 2, y: 2, z: 4, core: 2. Of those that a mesh axis runs over, the one named last changes fastest.
Arguments:
- column_profiles: bfloat16 [128, 100, 512], P('cols', None, 'mem'), may hold values from -6 to 6
- w_in: bfloat16 [100, 256], replicated, may hold values from -0.625 to 0.625
- w_depth: float32 [3, 256], replicated, may hold values from -3 to 3
- w_out: bfloat16 [256, 100], replicated, may hold values from -0.375 to 0.375
- obs_op: float32 [100, 16], replicated, may hold values from -0.625 to 0.625
- foot: int32 [1024, 4], P('cols'), may hold values from -1 to 15, as said below
- owner: int32 [1024, 1], P('cols'), may hold values from 0 to 7; in each aligned block of 128 rows (0 to 127, 128 to 255, ...) at most 32 rows name the same one
- obs: float32 [1024, 16], P('cols'), may hold values from -6 to 6
- rinv: float32 [1024, 16], P('cols'), may hold values from 0.5 to 4
- inflation: float32 [8], P('cols'), may hold values from 0.5 to 2
Outputs:
- analysis: bfloat16 [128, 100, 512], P('cols', None, 'mem')
The draws below stay inside these ranges and needn't reach their ends.
Inputs may be any that keep to these rules, and one draw needn't show every extreme that they name: `foot`: the first slot of every batch is a column of its source; other slots are a column or -1. Among the 128 batches of one index of cols, no owner appears more than 32 times.
All inputs are finite; a program needn't handle non-finite values.
Results may differ from the reference program's by a relative error of at most 0.01.
Values may be sent and summed in bfloat16 or wider, within the bound.
A program may use at most 64 MiB of HBM per device.

```python
import math
import jax
import jax.numpy as jnp
import numpy as np
from jax import lax

C = 100
HID = 256
ENSEMBLE_SIZE = 512
OBS = 16
FOOT = 4
COL_DEV = 16
SRC_B = 128
CAP = 32
NCOL = 128
NB = 1024
N_COLS = 8


def draw_foot(key, part):
    first_key, second_key = jax.random.split(jax.random.fold_in(key, 17))
    columns = jax.random.randint(first_key, (NB, FOOT), 0, COL_DEV)
    keep = jax.random.randint(second_key, (NB, FOOT), 0, 2)
    keep = keep.at[:, 0].set(1)
    return jnp.where(keep == 1, columns, -1).astype(jnp.int32)


def steps_of(rng, shape, cuts, low, high):
    gain, own = 1.0, jax.random.fold_in(rng, 6)
    for dim, blocks in cuts:
        draws = jnp.exp(jax.random.uniform(jax.random.fold_in(own, dim), (blocks,), jnp.float32, low / len(cuts), high / len(cuts)))
        gain = gain * jnp.repeat(draws, shape[dim] // blocks).reshape([-1 if axis == dim else 1 for axis in range(len(shape))])
    return gain


def assign_block(own_key, own, number, rows, number_of, top, bound, slope):
    ranking = jax.random.permutation(own_key, number_of)
    packed, usual = shares(number_of, rows * top, bound, slope, True), shares(number_of, rows * top, bound, slope, False)
    places = jnp.arange(number_of)

    def named(tallies, rotation):
        used = int((tallies > 0).sum())
        fixed = max(1, used // 4)
        passed = fixed + (places - fixed + rotation * (used - fixed)) % max(1, number_of - fixed)
        return jnp.zeros((number_of,), jnp.int32).at[ranking[jnp.where(places < fixed, places, passed)]].set(jnp.asarray(tallies, jnp.int32))

    tallies = jnp.where(number % 4 == 0, named(packed, number // 4), named(usual, number - number // 4 - 1))
    mixed = jax.random.permutation(jax.random.fold_in(own, 3), number_of)
    donor, receiver = mixed[0:number_of // 2 * 2:2], mixed[1:number_of // 2 * 2:2]
    room = jnp.minimum(tallies[donor] - 1, bound - tallies[receiver]) // 2
    room = jnp.where((donor == ranking[0]) | (receiver == ranking[0]) | (tallies[receiver] == 0), 0, jnp.maximum(room, 0))
    passed = jax.random.randint(jax.random.fold_in(own, 4), (number_of // 2,), 0, 1 << 20) % (room + 1)
    tallies = tallies.at[donor].add(-passed).at[receiver].add(passed)
    labels = jnp.searchsorted(jnp.cumsum(tallies), jnp.arange(rows * top), side="right").astype(jnp.int32)
    listing = labels.reshape(top, rows).T
    listing = listing[jax.random.permutation(jax.random.fold_in(own, 1), rows)]
    rotation = jax.random.randint(jax.random.fold_in(own, 2), (rows, 1), 0, top)
    return jnp.take_along_axis(listing, (jnp.arange(top)[None, :] + rotation) % top, axis=1)


def shares(number_of, total, bound, lean, full):
    loads = [(1 << 20) // math.isqrt(rank ** lean) + 1 for rank in range(1, number_of + 1)]
    largest = bound if full else min(bound, max(-(-total // number_of), total * loads[0] // sum(loads)))
    least = 1 if total - largest >= number_of - 1 else 0
    given, spare = [largest] + [least] * (number_of - 1), total - largest - least * (number_of - 1)
    while spare > 0:
        candidates = [i for i in range(1, number_of) if given[i] < largest] or [i for i in range(1, number_of) if given[i] < bound]
        pool, remaining = sum([loads[i] for i in candidates]), spare
        for i in candidates:
            addition = min(bound - given[i], max(1, remaining * loads[i] // pool), spare)
            given[i] = given[i] + addition
            spare = spare - addition
    return np.array(given)


def scatter_about(own_key, shape, scale, limit, cuts=(), kind=jnp.bfloat16):
    values = jax.random.normal(own_key, shape, jnp.float32) * scale
    if len(cuts) > 0:
        values = steps_of(own_key, shape, cuts, -0.22, 0.18) * values
    return jnp.clip(values, min=-limit, max=limit).astype(kind)


def setup_inputs(seed: int = 0) -> dict:
    key_of = jax.random.split(jax.random.key(seed), 11)
    column_profiles = scatter_about(key_of[0], (NCOL, C, ENSEMBLE_SIZE), 1.0, 6.0, ((0, 8), (2, 4)))
    w_in = scatter_about(key_of[1], (C, HID), C ** -0.5, 0.625)
    w_depth = scatter_about(key_of[2], (3, HID), 0.6, 3.0, (), jnp.float32)
    w_out = scatter_about(key_of[3], (HID, C), HID ** -0.5, 0.375)
    obs_op = scatter_about(key_of[4], (C, OBS), C ** -0.5, 0.625, (), jnp.float32)
    foot = draw_foot(jax.random.fold_in(key_of[10], 71), 0)
    owner_keys = jax.random.split(jax.random.fold_in(key_of[6], 1), NB // SRC_B)
    owner_turns = jax.random.permutation(jax.random.fold_in(key_of[6], 3), NB // SRC_B)
    owner = jax.vmap(lambda own, number: assign_block(jax.random.fold_in(key_of[6], 2), own, number, SRC_B, N_COLS, 1, CAP, 2))(owner_keys, owner_turns).reshape((NB, 1))
    obs = scatter_about(key_of[7], (NB, OBS), 1.0, 6.0, ((0, 8),), jnp.float32)
    rinv = jnp.clip(jnp.exp(math.log(4.0) - 2.0794415 * jax.random.uniform(key_of[8], (NB, OBS), jnp.float32) ** steps_of(key_of[8], (NB, OBS), ((0, 8),), -0.2, 0.2)), 0.5, 4.0)
    inflation = jnp.clip(jnp.exp(math.log(2.0) - 1.3862944 * jax.random.uniform(key_of[9], (N_COLS,), jnp.float32) ** steps_of(key_of[9], (N_COLS,), ((0, 8),), -0.2, 0.2)), 0.5, 2.0)
    return dict(column_profiles=column_profiles, w_in=w_in, w_depth=w_depth, w_out=w_out, obs_op=obs_op, foot=foot, owner=owner, obs=obs, rinv=rinv, inflation=inflation)


def reference(column_profiles, w_in, w_depth, w_out, obs_op, foot, owner, obs, rinv, inflation):
    top = lax.Precision.HIGHEST
    zeros = jnp.zeros((1, C, ENSEMBLE_SIZE), jnp.bfloat16)
    padded = jnp.concatenate([zeros, column_profiles, zeros], axis=0)

    def predicted_portion(input_profile):
        window = lax.dynamic_slice_in_dim(padded, input_profile * COL_DEV, COL_DEV + 2, 0)
        hidden = jax.nn.gelu(jnp.einsum('kcm,ch->khm', window.astype(jnp.float32), w_in.astype(jnp.float32), precision=top)).astype(jnp.bfloat16)
        mixed = (w_depth[0][None, :, None] * hidden[:-2] + w_depth[1][None, :, None] * hidden[1:-1] + w_depth[2][None, :, None] * hidden[2:]).astype(jnp.bfloat16)
        update = jnp.einsum('khm,hc->kcm', mixed.astype(jnp.float32), w_out.astype(jnp.float32), precision=top)
        return window[1:-1].astype(jnp.float32) + update
    predicted_column = lax.map(predicted_portion, jnp.arange(N_COLS, dtype=jnp.int32))
    profile_average = lax.optimization_barrier(jnp.sum(predicted_column, axis=3)) / ENSEMBLE_SIZE
    departure_from_average = predicted_column - profile_average[..., None]
    pobs = jnp.einsum('skcm,co->skom', departure_from_average, obs_op, precision=top)
    mobs = jnp.einsum('skc,co->sko', profile_average, obs_op, precision=top)
    foot3 = foot.reshape(N_COLS, SRC_B, FOOT)
    hits = (foot3[..., None] == jnp.arange(COL_DEV, dtype=jnp.int32)).astype(jnp.float32)
    counts = lax.optimization_barrier(jnp.sum((foot3 >= 0).astype(jnp.float32), axis=2))
    onehot = lax.optimization_barrier(jnp.sum(hits, axis=2)) / counts[..., None]
    fpert = jnp.einsum('sbk,skom->sbom', onehot, pobs, precision=top)
    fmean = jnp.einsum('sbk,sko->sbo', onehot, mobs, precision=top)
    scale = 1.0 / math.sqrt(ENSEMBLE_SIZE - 1)
    rinv3 = rinv.reshape(N_COLS, SRC_B, OBS)
    spread = (rinv3[..., None] * fpert * scale).astype(jnp.bfloat16).reshape(NB, OBS, ENSEMBLE_SIZE)
    innov = (rinv3 * (obs.reshape(N_COLS, SRC_B, OBS) - fmean)).astype(jnp.bfloat16).reshape(NB, OBS)
    factor = inflation[owner[:, 0]] ** 2
    spread32 = spread.astype(jnp.float32)
    weighted = spread32 * factor[:, None, None]
    gram = jnp.eye(ENSEMBLE_SIZE, dtype=jnp.float32) + jnp.einsum('bom,boj->mj', weighted, spread32, precision=top)
    vec = jnp.einsum('bom,bo->m', weighted, innov.astype(jnp.float32), precision=top)
    chol = jnp.linalg.cholesky(gram)
    weights = jax.scipy.linalg.cho_solve((chol, True), vec)
    tinv = jax.scipy.linalg.solve_triangular(chol.T, jnp.eye(ENSEMBLE_SIZE, dtype=jnp.float32), lower=False)
    mix_w = (weights[:, None] * scale + tinv).astype(jnp.bfloat16)
    pertb = departure_from_average.astype(jnp.bfloat16)

    def analyse(pair):
        mean_block, pert_block = pair
        moved = jnp.einsum('kcm,mj->kcj', pert_block.astype(jnp.float32), mix_w.astype(jnp.float32), precision=top)
        return (mean_block[:, :, None] + moved).astype(jnp.bfloat16)
    analysis = lax.map(analyse, (profile_average, pertb))
    return analysis.reshape(N_COLS * COL_DEV, C, ENSEMBLE_SIZE)
```

```python
import functools
import math

import jax
import jax.numpy as jnp
from jax import lax
from jax.experimental import pallas as pl
from jax.experimental.pallas import tpu as pltpu
from jax.sharding import PartitionSpec as P

TOP = lax.Precision.HIGHEST
F32 = jnp.float32
MESH = pl.DeviceIdType.MESH
VMEM = pl.BlockSpec(memory_space=pltpu.VMEM)


def remote(src, dst, send, recv, where):
    return pltpu.make_async_remote_copy(
        src_ref=src, dst_ref=dst, send_sem=send, recv_sem=recv,
        device_id=where, device_id_type=MESH,
    )


def mem_peers():
    m = lax.axis_index("mem")
    far = lax.rem(m + 2, 4)
    near = m + 1 - 2 * lax.rem(m, 2)
    return m, far, near


def edge_kernel(n_cols, first_ref, last_ref, factor_ref, low_ref, high_ref, factors_ref,
                low_buf, high_buf, factor_buf, edge_send, edge_recv, f_send, f_recv):
    c = lax.axis_index("cols")
    barrier = pltpu.get_barrier_semaphore()
    for d in range(1, n_cols):
        pl.semaphore_signal(barrier, inc=1, device_id={"cols": lax.rem(c + d, n_cols)}, device_id_type=MESH)
    pl.semaphore_wait(barrier, n_cols - 1)
    up = remote(last_ref, low_buf, edge_send.at[0], edge_recv.at[0], {"cols": lax.rem(c + 1, n_cols)})
    down = remote(first_ref, high_buf, edge_send.at[1], edge_recv.at[1], {"cols": lax.rem(c + n_cols - 1, n_cols)})
    up.start()
    down.start()
    copies = []
    for d in range(1, n_cols):
        copy = remote(factor_ref, factor_buf.at[d - 1], f_send.at[d - 1], f_recv.at[d - 1],
                      {"cols": lax.rem(c + d, n_cols)})
        copy.start()
        copies.append(copy)
    factors_ref[c] = factor_ref[...]
    for d in range(1, n_cols):
        copies[d - 1].wait()
        factors_ref[lax.rem(c + n_cols - d, n_cols)] = factor_buf[d - 1]
    up.wait()
    down.wait()
    low_ref[...] = jnp.where(c > 0, low_buf[...].astype(F32), 0.0).astype(low_ref.dtype)
    high_ref[...] = jnp.where(c < n_cols - 1, high_buf[...].astype(F32), 0.0).astype(high_ref.dtype)


def exchange_edges(first, last, factor, n_cols):
    count = n_cols - 1
    return pl.pallas_call(
        functools.partial(edge_kernel, n_cols),
        out_shape=(
            jax.ShapeDtypeStruct(first.shape, first.dtype),
            jax.ShapeDtypeStruct(first.shape, first.dtype),
            jax.ShapeDtypeStruct((n_cols,) + factor.shape, factor.dtype),
        ),
        in_specs=[VMEM] * 3,
        out_specs=(VMEM,) * 3,
        scratch_shapes=[
            pltpu.VMEM(first.shape, first.dtype),
            pltpu.VMEM(first.shape, first.dtype),
            pltpu.VMEM((count,) + factor.shape, factor.dtype),
            pltpu.SemaphoreType.DMA((2,)),
            pltpu.SemaphoreType.DMA((2,)),
            pltpu.SemaphoreType.DMA((count,)),
            pltpu.SemaphoreType.DMA((count,)),
        ],
        compiler_params=pltpu.CompilerParams(collective_id=0, has_side_effects=True, vmem_limit_bytes=16 << 20),
    )(first, last, factor)


def mem_kernel(seen_ref, sums_ref, all_ref, total_ref, seen_buf, sums_buf, send, recv):
    m, far, near = mem_peers()
    barrier = pltpu.get_barrier_semaphore()
    for peer in (far, near):
        pl.semaphore_signal(barrier, inc=1, device_id={"mem": peer}, device_id_type=MESH)
    pl.semaphore_wait(barrier, 2)
    copies = []
    for i, (src, buf) in enumerate(((sums_ref, sums_buf), (seen_ref, seen_buf))):
        a = remote(src, buf.at[0], send.at[i, 0], recv.at[i, 0], {"mem": far})
        b = remote(src, buf.at[1], send.at[i, 1], recv.at[i, 1], {"mem": near})
        a.start()
        b.start()
        copies.append((a, b))
    thirds = []
    for i, buf in enumerate((sums_buf, seen_buf)):
        copies[i][0].wait()
        t = remote(buf.at[0], buf.at[2], send.at[i, 2], recv.at[i, 2], {"mem": near})
        t.start()
        thirds.append(t)
    all_ref[m] = seen_ref[...]
    all_ref[far] = seen_buf[0]
    for i in range(2):
        copies[i][1].wait()
        thirds[i].wait()
    total_ref[...] = (sums_ref[...] + sums_buf[0]) + (sums_buf[1] + sums_buf[2])
    all_ref[near] = seen_buf[1]
    all_ref[lax.rem(near + 2, 4)] = seen_buf[2]


def exchange_mem(seen, sums):
    return pl.pallas_call(
        mem_kernel,
        out_shape=(
            jax.ShapeDtypeStruct((4,) + seen.shape, F32),
            jax.ShapeDtypeStruct(sums.shape, F32),
        ),
        in_specs=[VMEM] * 2,
        out_specs=(VMEM,) * 2,
        scratch_shapes=[
            pltpu.VMEM((3,) + seen.shape, F32),
            pltpu.VMEM((3,) + sums.shape, F32),
            pltpu.SemaphoreType.DMA((2, 3)),
            pltpu.SemaphoreType.DMA((2, 3)),
        ],
        compiler_params=pltpu.CompilerParams(collective_id=1, has_side_effects=True, vmem_limit_bytes=16 << 20),
    )(seen, sums)


def gram_kernel(n_cols, part_ref, vec_ref, gram_ref, total_ref, rbuf, vbuf, gbuf,
                r_send, r_recv, v_send, v_recv, g_send, g_recv,
                a_send, a_recv, b_send, b_recv, t_send, t_recv):
    c = lax.axis_index("cols")
    m, far, near = mem_peers()
    barrier = pltpu.get_barrier_semaphore()
    for d in range(1, n_cols):
        pl.semaphore_signal(barrier, inc=1, device_id={"cols": lax.rem(c + d, n_cols)}, device_id_type=MESH)
    for peer in (far, near):
        pl.semaphore_signal(barrier, inc=1, device_id={"mem": peer}, device_id_type=MESH)
    pl.semaphore_wait(barrier, n_cols + 1)
    rows, vecs = [], []
    for d in range(1, n_cols):
        peer = lax.rem(c + d, n_cols)
        copy = remote(part_ref.at[peer], rbuf.at[d - 1], r_send.at[d - 1], r_recv.at[d - 1], {"cols": peer})
        copy.start()
        rows.append(copy)
    for d in range(1, n_cols):
        peer = lax.rem(c + d, n_cols)
        copy = remote(vec_ref, vbuf.at[d - 1], v_send.at[d - 1], v_recv.at[d - 1], {"cols": peer})
        copy.start()
        vecs.append(copy)
    total = part_ref[c]
    for d in range(1, n_cols):
        rows[d - 1].wait()
        total = total + rbuf[d - 1]
    gbuf[m, c] = total
    spread_out = []
    for d in range(1, n_cols):
        copy = remote(gbuf.at[m, c], gbuf.at[m, c], g_send.at[d - 1], g_recv.at[d - 1],
                      {"cols": lax.rem(c + d, n_cols)})
        copy.start()
        spread_out.append(copy)
    pairs = []
    for d in range(n_cols):
        held = lax.rem(c + n_cols - d, n_cols)
        if d > 0:
            spread_out[d - 1].wait_recv()
        a = remote(gbuf.at[m, held], gbuf.at[m, held], a_send.at[d], a_recv.at[d], {"mem": far})
        b = remote(gbuf.at[m, held], gbuf.at[m, held], b_send.at[d], b_recv.at[d], {"mem": near})
        a.start()
        b.start()
        pairs.append((a, b))
    thirds = []
    for d in range(n_cols):
        held = lax.rem(c + n_cols - d, n_cols)
        pairs[d][0].wait_recv()
        t = remote(gbuf.at[far, held], gbuf.at[far, held], t_send.at[d], t_recv.at[d], {"mem": near})
        t.start()
        thirds.append(t)
    whole = vec_ref[...]
    for d in range(1, n_cols):
        vecs[d - 1].wait()
        whole = whole + vbuf[d - 1]
    total_ref[...] = whole
    for d in range(n_cols):
        pairs[d][1].wait_recv()
        thirds[d].wait_recv()
    for d in range(1, n_cols):
        spread_out[d - 1].wait_send()
    for d in range(n_cols):
        pairs[d][0].wait_send()
        pairs[d][1].wait_send()
        thirds[d].wait_send()
    gram_ref[...] = gbuf[...]


def exchange_gram(part, vec, n_cols):
    count = n_cols - 1
    dma = pltpu.SemaphoreType.DMA
    slab = part.shape[1:]
    return pl.pallas_call(
        functools.partial(gram_kernel, n_cols),
        out_shape=(
            jax.ShapeDtypeStruct((4, n_cols) + slab, F32),
            jax.ShapeDtypeStruct(vec.shape, F32),
        ),
        in_specs=[VMEM] * 2,
        out_specs=(VMEM,) * 2,
        scratch_shapes=[
            pltpu.VMEM((count,) + slab, F32),
            pltpu.VMEM((count,) + vec.shape, F32),
            pltpu.VMEM((4, n_cols) + slab, F32),
        ] + [dma((count,))] * 6 + [dma((n_cols,))] * 6,
        compiler_params=pltpu.CompilerParams(collective_id=2, has_side_effects=True, vmem_limit_bytes=16 << 20),
    )(part, vec)


def lane_copy(x, j):
    return jnp.take_along_axis(x, jnp.full(x.shape, j, jnp.int32), axis=1)


def eliminate(block, width):
    lane = lax.broadcasted_iota(jnp.int32, (8, width), 1)
    sub = lax.broadcasted_iota(jnp.int32, (8, width), 0)
    for p in range(width // 8):
        row = block[p]
        base = 8 * p
        cols = [lane_copy(row, base + k) for k in range(8)]
        recips, tops = [], []
        for j in range(8):
            recip = 1.0 / cols[j][j:j + 1]
            mult = jnp.where(sub > j, cols[j] * recip, 0.0)
            top = {}
            for k in range(j + 1, 8):
                top[k] = cols[k][j:j + 1]
                cols[k] = cols[k] - mult * top[k]
            recips.append(recip)
            tops.append(top)
            row = jnp.where((lane == base + j) & (sub > j), -mult, row - mult * row[j:j + 1])
        block[p] = row
        for q in range(p + 1, width // 8):
            x = block[q]
            below = [lane_copy(x, base + k) for k in range(8)]
            for j in range(8):
                mult = below[j] * recips[j]
                for k in range(j + 1, 8):
                    below[k] = below[k] - mult * tops[j][k]
                x = jnp.where(lane == base + j, -mult, x - mult * row[j:j + 1])
            block[q] = x
    return block


def factor_kernel(scale, first_ref, gram_ref, vec_ref, mix_ref, w_ref):
    width = 128
    order = gram_ref.shape[0]
    blocks = order // width
    w_ref[...] = gram_ref[...]
    lane = lax.broadcasted_iota(jnp.int32, (8, width), 1)
    sub = lax.broadcasted_iota(jnp.int32, (8, width), 0)

    def step(b, carry):
        o = pl.multiple_of(b * width, width)
        block = [
            w_ref[pl.ds(o + 8 * i, 8), pl.ds(o, width)] + jnp.where((lane == sub + 8 * i) , 1.0, 0.0)
            for i in range(width // 8)
        ]
        block = eliminate(block, width)
        rows = []
        for i in range(width // 8):
            diag = lane == sub + 8 * i
            root = lax.rsqrt(jnp.sum(jnp.where(diag, block[i], 0.0), axis=1, keepdims=True))
            rows.append(jnp.where(diag, root, jnp.where(lane < sub + 8 * i, block[i] * root, 0.0)))
        inverse = jnp.concatenate(rows, axis=0)
        solved = jnp.dot(inverse, w_ref[pl.ds(o, width), :], precision=TOP, preferred_element_type=F32)
        w_ref[pl.ds(o, width), :] = solved
        w_ref[pl.ds(o, width), pl.ds(o, width)] = inverse

        def update(t, inner):
            u = pl.multiple_of(t * width, width)
            upper = w_ref[pl.ds(o, width), pl.ds(u, width)]
            product = lax.dot_general(
                upper, w_ref[pl.ds(o, width), :], (((0,), (0,)), ((), ())),
                precision=TOP, preferred_element_type=F32,
            )
            w_ref[pl.ds(u, width), pl.ds(o, width)] = jnp.zeros((width, width), F32)
            w_ref[pl.ds(u, width), :] -= product
            return inner

        lax.fori_loop(b + 1, blocks, update, 0)
        return carry

    lax.fori_loop(0, blocks, step, 0)
    row_id = lax.broadcasted_iota(jnp.int32, (order, order), 0)
    col_id = lax.broadcasted_iota(jnp.int32, (order, order), 1)
    chol_inverse = jnp.where(row_id >= col_id, w_ref[...], 0.0)
    w_ref[...] = chol_inverse
    half = jnp.sum(chol_inverse * vec_ref[...], axis=1, keepdims=True)
    weights = jnp.sum(chol_inverse * half, axis=0, keepdims=True)
    mine = w_ref[pl.ds(pl.multiple_of(first_ref[0] * width, width), mix_ref.shape[0]), :]
    mix_ref[...] = (weights * scale + mine).astype(mix_ref.dtype)


def factor(first, gram, vec, rows, scale):
    order = gram.shape[0]
    return pl.pallas_call(
        functools.partial(factor_kernel, scale),
        out_shape=jax.ShapeDtypeStruct((rows, order), jnp.bfloat16),
        in_specs=[pl.BlockSpec(memory_space=pltpu.SMEM), VMEM, VMEM],
        out_specs=VMEM,
        scratch_shapes=[pltpu.VMEM((order, order), F32)],
        compiler_params=pltpu.CompilerParams(vmem_limit_bytes=32 << 20),
        cost_estimate=pl.CostEstimate(flops=40_000_000_000, bytes_accessed=1 << 22, transcendentals=0),
    )(first, gram, vec)


def body(column_profiles, w_in, w_depth, w_out, obs_op, foot, owner, obs, rinv, inflation):
    n_cols = lax.axis_size("cols")
    n_mem = lax.axis_size("mem")
    col_dev, channels, mem_dev = column_profiles.shape
    n_obs = obs.shape[1]
    members = mem_dev * n_mem
    direct = n_cols <= 8 and n_mem == 4
    scale = 1.0 / math.sqrt(members - 1)

    hidden = jax.nn.gelu(
        jnp.einsum("kcm,ch->khm", column_profiles, w_in, preferred_element_type=F32)
    ).astype(jnp.bfloat16)
    if direct:
        low, high, gains = exchange_edges(
            hidden[0], hidden[-1], jnp.broadcast_to(inflation[:, None], (8, 128)), n_cols
        )
        low, high, gains = low[None], high[None], gains[:, 0, 0]
    else:
        forward = [(i, i + 1) for i in range(n_cols - 1)]
        low = lax.ppermute(hidden[-1:], "cols", forward)
        high = lax.ppermute(hidden[:1], "cols", [(t, s) for s, t in forward])
        gains = lax.all_gather(inflation, "cols", axis=0, tiled=True)
    hidden = jnp.concatenate([low, hidden, high], axis=0)
    mixed = (
        w_depth[0][None, :, None] * hidden[:-2]
        + w_depth[1][None, :, None] * hidden[1:-1]
        + w_depth[2][None, :, None] * hidden[2:]
    ).astype(jnp.bfloat16)
    forecast = column_profiles.astype(F32) + jnp.einsum(
        "khm,hc->kcm", mixed, w_out, preferred_element_type=F32
    )
    sums = jnp.sum(forecast, axis=2)
    seen = jnp.einsum("kcm,co->kom", forecast, obs_op, precision=TOP).reshape(col_dev * n_obs, mem_dev)
    if direct:
        seen_all, sums = exchange_mem(seen, sums)
    else:
        seen_all = lax.all_gather(seen, "mem", axis=0)
        sums = lax.psum(sums, "mem")
    mean = sums / members
    pert = (forecast - mean[:, :, None]).astype(jnp.bfloat16)
    pert_all = lax.all_gather(pert, "mem", axis=2, tiled=True)
    mobs = jnp.dot(mean, obs_op, precision=TOP)
    seen_all = seen_all - mobs.reshape(1, col_dev * n_obs, 1)
    seen = seen - mobs.reshape(col_dev * n_obs, 1)

    hits = (foot[:, :, None] == jnp.arange(col_dev, dtype=jnp.int32)[None, None, :]).astype(F32)
    counts = jnp.sum((foot >= 0).astype(F32), axis=1)
    onehot = jnp.sum(hits, axis=1) / counts[:, None]
    fmean = jnp.dot(onehot, mobs, precision=TOP)
    innov = (rinv * (obs - fmean)).astype(jnp.bfloat16).astype(F32)
    table = (owner == jnp.arange(n_cols, dtype=jnp.int32)[None, :]).astype(F32)
    chosen = jnp.sum(table * gains[None, :], axis=1)
    batch = foot.shape[0]
    load = (onehot[:, :, None] * (rinv * (chosen * scale)[:, None])[:, None, :]).reshape(batch, col_dev * n_obs)
    kind = jnp.arange(col_dev * n_obs, dtype=jnp.int32) % n_obs
    link = jnp.dot(load.T, load, precision=TOP) * (kind[:, None] == kind[None, :]).astype(F32)
    pull = jnp.sum(
        load * jnp.broadcast_to((innov * chosen[:, None])[:, None, :], (batch, col_dev, n_obs)).reshape(load.shape),
        axis=0,
    )
    mine = jnp.dot(link, seen, precision=TOP)
    part = jnp.einsum("qm,nqj->mnj", mine, seen_all, precision=TOP).reshape(mem_dev, members)
    vec = jnp.einsum("q,nqj->nj", pull, seen_all, precision=TOP)
    if direct:
        gram, vec = exchange_gram(part.reshape(n_cols, mem_dev // n_cols, members), vec, n_cols)
        gram = gram.reshape(members, members)
    else:
        part, vec = lax.psum((part, vec), "cols")
        gram = lax.all_gather(part, "mem", axis=0, tiled=True)
    first = lax.axis_index("mem").astype(jnp.int32)[None]
    mix = factor(first, gram, vec.reshape(1, members), mem_dev, scale)
    moved = jnp.einsum("kcm,jm->kcj", pert_all, mix, preferred_element_type=F32)
    return (mean[:, :, None] + moved).astype(jnp.bfloat16)


def solution(mesh):
    placed = (
        P("cols", None, "mem"),
        P(),
        P(),
        P(),
        P(),
        P("cols", None),
        P("cols", None),
        P("cols", None),
        P("cols", None),
        P("cols"),
    )
    return jax.shard_map(
        body, mesh=mesh, in_specs=placed, out_specs=P("cols", None, "mem"), check_vma=False
    )
```

```python
import functools
import math

import jax
import jax.numpy as jnp
from jax import lax
from jax.experimental import pallas as pl
from jax.experimental.pallas import tpu as pltpu
from jax.sharding import PartitionSpec as P

TOP = lax.Precision.HIGHEST
F32 = jnp.float32
MESH = pl.DeviceIdType.MESH
VMEM = pl.BlockSpec(memory_space=pltpu.VMEM)


def remote(src, dst, send, recv, where):
    return pltpu.make_async_remote_copy(
        src_ref=src, dst_ref=dst, send_sem=send, recv_sem=recv,
        device_id=where, device_id_type=MESH,
    )


def mem_peers():
    m = lax.axis_index("mem")
    far = lax.rem(m + 2, 4)
    near = m + 1 - 2 * lax.rem(m, 2)
    return m, far, near


def edge_kernel(n_cols, first_ref, last_ref, factor_ref, low_ref, high_ref, factors_ref,
                low_buf, high_buf, factor_buf, edge_send, edge_recv, f_send, f_recv):
    c = lax.axis_index("cols")
    barrier = pltpu.get_barrier_semaphore()
    for d in range(1, n_cols):
        pl.semaphore_signal(barrier, inc=1, device_id={"cols": lax.rem(c + d, n_cols)}, device_id_type=MESH)
    pl.semaphore_wait(barrier, n_cols - 1)
    up = remote(last_ref, low_buf, edge_send.at[0], edge_recv.at[0], {"cols": lax.rem(c + 1, n_cols)})
    down = remote(first_ref, high_buf, edge_send.at[1], edge_recv.at[1], {"cols": lax.rem(c + n_cols - 1, n_cols)})
    up.start()
    down.start()
    copies = []
    for d in range(1, n_cols):
        copy = remote(factor_ref, factor_buf.at[d - 1], f_send.at[d - 1], f_recv.at[d - 1],
                      {"cols": lax.rem(c + d, n_cols)})
        copy.start()
        copies.append(copy)
    factors_ref[c] = factor_ref[...]
    for d in range(1, n_cols):
        copies[d - 1].wait()
        factors_ref[lax.rem(c + n_cols - d, n_cols)] = factor_buf[d - 1]
    up.wait()
    down.wait()
    low_ref[...] = jnp.where(c > 0, low_buf[...].astype(F32), 0.0).astype(low_ref.dtype)
    high_ref[...] = jnp.where(c < n_cols - 1, high_buf[...].astype(F32), 0.0).astype(high_ref.dtype)


def exchange_edges(first, last, factor, n_cols):
    count = n_cols - 1
    return pl.pallas_call(
        functools.partial(edge_kernel, n_cols),
        out_shape=(
            jax.ShapeDtypeStruct(first.shape, first.dtype),
            jax.ShapeDtypeStruct(first.shape, first.dtype),
            jax.ShapeDtypeStruct((n_cols,) + factor.shape, factor.dtype),
        ),
        in_specs=[VMEM] * 3,
        out_specs=(VMEM,) * 3,
        scratch_shapes=[
            pltpu.VMEM(first.shape, first.dtype),
            pltpu.VMEM(first.shape, first.dtype),
            pltpu.VMEM((count,) + factor.shape, factor.dtype),
            pltpu.SemaphoreType.DMA((2,)),
            pltpu.SemaphoreType.DMA((2,)),
            pltpu.SemaphoreType.DMA((count,)),
            pltpu.SemaphoreType.DMA((count,)),
        ],
        compiler_params=pltpu.CompilerParams(collective_id=0, has_side_effects=True, vmem_limit_bytes=16 << 20),
    )(first, last, factor)


def mem_kernel(seen_ref, sums_ref, all_ref, total_ref, seen_buf, sums_buf, send, recv):
    m, far, near = mem_peers()
    barrier = pltpu.get_barrier_semaphore()
    for peer in (far, near):
        pl.semaphore_signal(barrier, inc=1, device_id={"mem": peer}, device_id_type=MESH)
    pl.semaphore_wait(barrier, 2)
    copies = []
    for i, (src, buf) in enumerate(((sums_ref, sums_buf), (seen_ref, seen_buf))):
        a = remote(src, buf.at[0], send.at[i, 0], recv.at[i, 0], {"mem": far})
        b = remote(src, buf.at[1], send.at[i, 1], recv.at[i, 1], {"mem": near})
        a.start()
        b.start()
        copies.append((a, b))
    thirds = []
    for i, buf in enumerate((sums_buf, seen_buf)):
        copies[i][0].wait()
        t = remote(buf.at[0], buf.at[2], send.at[i, 2], recv.at[i, 2], {"mem": near})
        t.start()
        thirds.append(t)
    all_ref[0] = seen_ref[...]
    all_ref[2] = seen_buf[0]
    for i in range(2):
        copies[i][1].wait()
        thirds[i].wait()
    total_ref[...] = (sums_ref[...] + sums_buf[0]) + (sums_buf[1] + sums_buf[2])
    turn = lax.rem(near - m + 4, 4)
    all_ref[turn] = seen_buf[1]
    all_ref[4 - turn] = seen_buf[2]


def exchange_mem(seen, sums):
    return pl.pallas_call(
        mem_kernel,
        out_shape=(
            jax.ShapeDtypeStruct((4,) + seen.shape, F32),
            jax.ShapeDtypeStruct(sums.shape, F32),
        ),
        in_specs=[VMEM] * 2,
        out_specs=(VMEM,) * 2,
        scratch_shapes=[
            pltpu.VMEM((3,) + seen.shape, F32),
            pltpu.VMEM((3,) + sums.shape, F32),
            pltpu.SemaphoreType.DMA((2, 3)),
            pltpu.SemaphoreType.DMA((2, 3)),
        ],
        compiler_params=pltpu.CompilerParams(collective_id=1, has_side_effects=True, vmem_limit_bytes=16 << 20),
    )(seen, sums)


def gram_kernel(n_cols, part_ref, vec_ref, pert_ref, gram_ref, total_ref, others_ref, rbuf, vbuf, gbuf, pbuf,
                p_send, p_recv,
                r_send, r_recv, v_send, v_recv, g_send, g_recv,
                a_send, a_recv, b_send, b_recv, t_send, t_recv):
    c = lax.axis_index("cols")
    m, far, near = mem_peers()
    barrier = pltpu.get_barrier_semaphore()
    for d in range(1, n_cols):
        pl.semaphore_signal(barrier, inc=1, device_id={"cols": lax.rem(c + d, n_cols)}, device_id_type=MESH)
    for peer in (far, near):
        pl.semaphore_signal(barrier, inc=1, device_id={"mem": peer}, device_id_type=MESH)
    pl.semaphore_wait(barrier, n_cols + 1)
    rows, vecs = [], []
    for d in range(1, n_cols):
        peer = lax.rem(c + d, n_cols)
        copy = remote(part_ref.at[peer], rbuf.at[d - 1], r_send.at[d - 1], r_recv.at[d - 1], {"cols": peer})
        copy.start()
        rows.append(copy)
    pert_far = remote(pert_ref, pbuf.at[0], p_send.at[0], p_recv.at[0], {"mem": far})
    pert_near = remote(pert_ref, pbuf.at[1], p_send.at[1], p_recv.at[1], {"mem": near})
    pert_far.start()
    pert_near.start()
    for d in range(1, n_cols):
        peer = lax.rem(c + d, n_cols)
        copy = remote(vec_ref, vbuf.at[d - 1], v_send.at[d - 1], v_recv.at[d - 1], {"cols": peer})
        copy.start()
        vecs.append(copy)
    total = part_ref[c]
    for d in range(1, n_cols):
        rows[d - 1].wait()
        total = total + rbuf[d - 1]
    gbuf[m, c] = total
    spread_out = []
    for d in range(1, n_cols):
        copy = remote(gbuf.at[m, c], gbuf.at[m, c], g_send.at[d - 1], g_recv.at[d - 1],
                      {"cols": lax.rem(c + d, n_cols)})
        copy.start()
        spread_out.append(copy)
    pairs = []
    for d in range(n_cols):
        held = lax.rem(c + n_cols - d, n_cols)
        if d > 0:
            spread_out[d - 1].wait_recv()
        a = remote(gbuf.at[m, held], gbuf.at[m, held], a_send.at[d], a_recv.at[d], {"mem": far})
        b = remote(gbuf.at[m, held], gbuf.at[m, held], b_send.at[d], b_recv.at[d], {"mem": near})
        a.start()
        b.start()
        pairs.append((a, b))
    pert_far.wait()
    pert_third = remote(pbuf.at[0], pbuf.at[2], p_send.at[2], p_recv.at[2], {"mem": near})
    pert_third.start()
    thirds = []
    for d in range(n_cols):
        held = lax.rem(c + n_cols - d, n_cols)
        pairs[d][0].wait_recv()
        t = remote(gbuf.at[far, held], gbuf.at[far, held], t_send.at[d], t_recv.at[d], {"mem": near})
        t.start()
        thirds.append(t)
    whole = vec_ref[...]
    for d in range(1, n_cols):
        vecs[d - 1].wait()
        whole = whole + vbuf[d - 1]
    for i in range(4):
        total_ref[lax.rem(m + i, 4)] = whole[i]
    for d in range(n_cols):
        pairs[d][1].wait_recv()
        thirds[d].wait_recv()
    for d in range(1, n_cols):
        spread_out[d - 1].wait_send()
    for d in range(n_cols):
        pairs[d][0].wait_send()
        pairs[d][1].wait_send()
        thirds[d].wait_send()
    gram_ref[...] = gbuf[...]
    pert_near.wait()
    pert_third.wait()
    others_ref[...] = pbuf[...]


def exchange_gram(part, vec, pert, n_cols):
    count = n_cols - 1
    dma = pltpu.SemaphoreType.DMA
    slab = part.shape[1:]
    return pl.pallas_call(
        functools.partial(gram_kernel, n_cols),
        out_shape=(
            jax.ShapeDtypeStruct((4, n_cols) + slab, F32),
            jax.ShapeDtypeStruct(vec.shape, F32),
            jax.ShapeDtypeStruct((3,) + pert.shape, pert.dtype),
        ),
        in_specs=[VMEM] * 3,
        out_specs=(VMEM,) * 3,
        scratch_shapes=[
            pltpu.VMEM((count,) + slab, F32),
            pltpu.VMEM((count,) + vec.shape, F32),
            pltpu.VMEM((4, n_cols) + slab, F32),
            pltpu.VMEM((3,) + pert.shape, pert.dtype),
            dma((3,)),
            dma((3,)),
        ] + [dma((count,))] * 6 + [dma((n_cols,))] * 6,
        compiler_params=pltpu.CompilerParams(collective_id=2, has_side_effects=True, vmem_limit_bytes=16 << 20),
    )(part, vec, pert)


def lane_copy(x, j):
    return jnp.take_along_axis(x, jnp.full(x.shape, j, jnp.int32), axis=1)


def eliminate(block, width):
    lane = lax.broadcasted_iota(jnp.int32, (8, width), 1)
    sub = lax.broadcasted_iota(jnp.int32, (8, width), 0)
    for p in range(width // 8):
        row = block[p]
        base = 8 * p
        cols = [lane_copy(row, base + k) for k in range(8)]
        recips, tops = [], []
        for j in range(8):
            recip = 1.0 / cols[j][j:j + 1]
            mult = jnp.where(sub > j, cols[j] * recip, 0.0)
            top = {}
            for k in range(j + 1, 8):
                top[k] = cols[k][j:j + 1]
                cols[k] = cols[k] - mult * top[k]
            recips.append(recip)
            tops.append(top)
            row = jnp.where((lane == base + j) & (sub > j), -mult, row - mult * row[j:j + 1])
        block[p] = row
        for q in range(p + 1, width // 8):
            x = block[q]
            below = [lane_copy(x, base + k) for k in range(8)]
            for j in range(8):
                mult = below[j] * recips[j]
                for k in range(j + 1, 8):
                    below[k] = below[k] - mult * tops[j][k]
                x = jnp.where(lane == base + j, -mult, x - mult * row[j:j + 1])
            block[q] = x
    return block


def factor_kernel(scale, first_ref, gram_ref, vec_ref, *rest):
    if len(rest) == 6:
        pert_ref, others_ref, mean_ref, out_ref, w_ref, mix_ref = rest
    else:
        pert_ref, (mix_ref, w_ref) = None, rest
    width = 128
    order = w_ref.shape[0]
    blocks = order // width
    if len(gram_ref.shape) == 2:
        w_ref[...] = gram_ref[...]
    else:
        for r in range(4):
            for t in range(min(3, 4 - r)):
                at = (r + t) * width
                w_ref[r * width:(r + 1) * width, at:at + width] = gram_ref[r, :, t * width:(t + 1) * width]
        w_ref[0:width, 3 * width:] = gram_ref[3, :, width:2 * width].T
    lane = lax.broadcasted_iota(jnp.int32, (8, width), 1)
    sub = lax.broadcasted_iota(jnp.int32, (8, width), 0)

    def step(b, carry):
        o = pl.multiple_of(b * width, width)
        block = [
            w_ref[pl.ds(o + 8 * i, 8), pl.ds(o, width)] + jnp.where((lane == sub + 8 * i) , 1.0, 0.0)
            for i in range(width // 8)
        ]
        block = eliminate(block, width)
        rows = []
        for i in range(width // 8):
            diag = lane == sub + 8 * i
            root = lax.rsqrt(jnp.sum(jnp.where(diag, block[i], 0.0), axis=1, keepdims=True))
            rows.append(jnp.where(diag, root, jnp.where(lane < sub + 8 * i, block[i] * root, 0.0)))
        inverse = jnp.concatenate(rows, axis=0)
        solved = jnp.dot(inverse, w_ref[pl.ds(o, width), :], precision=TOP, preferred_element_type=F32)
        w_ref[pl.ds(o, width), :] = solved
        w_ref[pl.ds(o, width), pl.ds(o, width)] = inverse

        def update(t, inner):
            u = pl.multiple_of(t * width, width)
            upper = w_ref[pl.ds(o, width), pl.ds(u, width)]
            product = lax.dot_general(
                upper, w_ref[pl.ds(o, width), :], (((0,), (0,)), ((), ())),
                precision=TOP, preferred_element_type=F32,
            )
            w_ref[pl.ds(u, width), pl.ds(o, width)] = jnp.zeros((width, width), F32)
            w_ref[pl.ds(u, width), :] -= product
            return inner

        lax.fori_loop(b + 1, blocks, update, 0)
        return carry

    lax.fori_loop(0, blocks, step, 0)
    row_id = lax.broadcasted_iota(jnp.int32, (order, order), 0)
    col_id = lax.broadcasted_iota(jnp.int32, (order, order), 1)
    chol_inverse = jnp.where(row_id >= col_id, w_ref[...], 0.0)
    w_ref[...] = chol_inverse
    half = jnp.sum(chol_inverse * vec_ref[...], axis=1, keepdims=True)
    weights = jnp.sum(chol_inverse * half, axis=0, keepdims=True)
    mine = w_ref[pl.ds(pl.multiple_of(first_ref[0] * width, width), mix_ref.shape[0]), :]
    mix_ref[...] = (weights * scale + mine).astype(mix_ref.dtype)
    if pert_ref is None:
        return
    m = first_ref[0]
    near = m + 1 - 2 * lax.rem(m, 2)
    sources = ((pert_ref[...], m), (others_ref[0], lax.rem(m + 2, 4)), (others_ref[1], near), (others_ref[2], lax.rem(near + 2, 4)))
    moved = None
    for source, place in sources:
        weight = mix_ref[:, pl.ds(pl.multiple_of(place * width, width), width)]
        term = lax.dot_general(source, weight, (((1,), (1,)), ((), ())), preferred_element_type=F32)
        moved = term if moved is None else moved + term
    mean = mean_ref[...]
    col_dev = mean.shape[0]
    for c in range(mean.shape[1]):
        out_ref[c] = (moved[c * col_dev:(c + 1) * col_dev] + mean[:, c:c + 1]).astype(out_ref.dtype)


def analyse(first, gram, vec, pert, others, mean, rows, scale):
    order = vec.shape[1]
    col_dev, channels = mean.shape
    return pl.pallas_call(
        functools.partial(factor_kernel, scale),
        out_shape=jax.ShapeDtypeStruct((channels, col_dev, rows), jnp.bfloat16),
        in_specs=[pl.BlockSpec(memory_space=pltpu.SMEM)] + [VMEM] * 5,
        out_specs=VMEM,
        scratch_shapes=[pltpu.VMEM((order, order), F32), pltpu.VMEM((rows, order), jnp.bfloat16)],
        compiler_params=pltpu.CompilerParams(vmem_limit_bytes=32 << 20),
    )(first, gram, vec, pert, others, mean)


def factor(first, gram, vec, rows, scale):
    order = vec.shape[1]
    return pl.pallas_call(
        functools.partial(factor_kernel, scale),
        out_shape=jax.ShapeDtypeStruct((rows, order), jnp.bfloat16),
        in_specs=[pl.BlockSpec(memory_space=pltpu.SMEM), VMEM, VMEM],
        out_specs=VMEM,
        scratch_shapes=[pltpu.VMEM((order, order), F32)],
        compiler_params=pltpu.CompilerParams(vmem_limit_bytes=32 << 20),
        cost_estimate=pl.CostEstimate(flops=40_000_000_000, bytes_accessed=1 << 22, transcendentals=0),
    )(first, gram, vec)


def body(column_profiles, w_in, w_depth, w_out, obs_op, foot, owner, obs, rinv, inflation):
    n_cols = lax.axis_size("cols")
    n_mem = lax.axis_size("mem")
    col_dev, channels, mem_dev = column_profiles.shape
    n_obs = obs.shape[1]
    members = mem_dev * n_mem
    direct = n_cols <= 8 and n_mem == 4 and mem_dev == 128
    scale = 1.0 / math.sqrt(members - 1)

    hidden = jax.nn.gelu(
        jnp.einsum("kcm,ch->khm", column_profiles, w_in, preferred_element_type=F32)
    ).astype(jnp.bfloat16)
    if direct:
        low, high, gains = exchange_edges(
            hidden[0], hidden[-1], jnp.broadcast_to(inflation[:, None], (8, 128)), n_cols
        )
        low, high, gains = low[None], high[None], gains[:, 0, 0]
    else:
        forward = [(i, i + 1) for i in range(n_cols - 1)]
        low = lax.ppermute(hidden[-1:], "cols", forward)
        high = lax.ppermute(hidden[:1], "cols", [(t, s) for s, t in forward])
        gains = lax.all_gather(inflation, "cols", axis=0, tiled=True)
    hidden = jnp.concatenate([low, hidden, high], axis=0)
    mixed = (
        w_depth[0][None, :, None] * hidden[:-2]
        + w_depth[1][None, :, None] * hidden[1:-1]
        + w_depth[2][None, :, None] * hidden[2:]
    ).astype(jnp.bfloat16)
    forecast = column_profiles.astype(F32) + jnp.einsum(
        "khm,hc->kcm", mixed, w_out, preferred_element_type=F32
    )
    sums = jnp.sum(forecast, axis=2)
    seen = jnp.einsum("kcm,co->kom", forecast, obs_op, precision=TOP).reshape(col_dev * n_obs, mem_dev)
    if direct:
        seen_all, sums = exchange_mem(seen, sums)
    else:
        seen_all = lax.all_gather(seen, "mem", axis=0)
        sums = lax.psum(sums, "mem")
    mean = sums / members
    pert = (forecast - mean[:, :, None]).astype(jnp.bfloat16)
    if direct:
        pert = jnp.transpose(pert, (1, 0, 2)).reshape(channels * col_dev, mem_dev)
    else:
        pert_all = lax.all_gather(pert, "mem", axis=2, tiled=True)
    mobs = jnp.dot(mean, obs_op, precision=TOP)
    seen_all = seen_all - mobs.reshape(1, col_dev * n_obs, 1)
    seen = seen - mobs.reshape(col_dev * n_obs, 1)

    hits = (foot[:, :, None] == jnp.arange(col_dev, dtype=jnp.int32)[None, None, :]).astype(F32)
    counts = jnp.sum((foot >= 0).astype(F32), axis=1)
    onehot = jnp.sum(hits, axis=1) / counts[:, None]
    fmean = jnp.dot(onehot, mobs, precision=TOP)
    innov = (rinv * (obs - fmean)).astype(jnp.bfloat16).astype(F32)
    table = (owner == jnp.arange(n_cols, dtype=jnp.int32)[None, :]).astype(F32)
    chosen = jnp.sum(table * gains[None, :], axis=1)
    batch = foot.shape[0]
    load = (onehot[:, :, None] * (rinv * (chosen * scale)[:, None])[:, None, :]).reshape(batch, col_dev * n_obs)
    kind = jnp.arange(col_dev * n_obs, dtype=jnp.int32) % n_obs
    link = jnp.dot(load.T, load, precision=TOP) * (kind[:, None] == kind[None, :]).astype(F32)
    pull = jnp.sum(
        load * jnp.broadcast_to((innov * chosen[:, None])[:, None, :], (batch, col_dev, n_obs)).reshape(load.shape),
        axis=0,
    )
    mine = jnp.dot(link, seen, precision=TOP)
    used = seen_all[:3] if direct else seen_all
    part = jnp.einsum("qm,nqj->mnj", mine, used, precision=TOP).reshape(mem_dev, -1)
    vec = jnp.einsum("q,nqj->nj", pull, seen_all, precision=TOP)
    if direct:
        gram, vec, others = exchange_gram(part.reshape(n_cols, mem_dev // n_cols, -1), vec, pert, n_cols)
        gram = gram.reshape(n_mem, mem_dev, -1)
    else:
        part, vec = lax.psum((part, vec), "cols")
        gram = lax.all_gather(part, "mem", axis=0, tiled=True)
    first = lax.axis_index("mem").astype(jnp.int32)[None]
    if direct:
        out = analyse(first, gram, vec.reshape(1, members), pert, others, mean, mem_dev, scale)
        return jnp.transpose(out, (1, 0, 2))
    mix = factor(first, gram, vec.reshape(1, members), mem_dev, scale)
    moved = jnp.einsum("kcm,jm->kcj", pert_all, mix, preferred_element_type=F32)
    return (mean[:, :, None] + moved).astype(jnp.bfloat16)


def solution(mesh):
    placed = (
        P("cols", None, "mem"),
        P(),
        P(),
        P(),
        P(),
        P("cols", None),
        P("cols", None),
        P("cols", None),
        P("cols", None),
        P("cols"),
    )
    return jax.shard_map(
        body, mesh=mesh, in_specs=placed, out_specs=P("cols", None, "mem"), check_vma=False
    )
```
